256 devices in a mesh: grid: 16 (over z_hi, y, core), band: 16 (over x, z_lo).
Axes of the slice: x: 4, y: 4, z: 8 (z_hi: 2, z_lo: 4; z = z_hi * 4 + z_lo), core: 2. Of those that a mesh axis runs over, the one named last changes fastest.
Arguments:
- states: bfloat16 [24576, 32768], P('grid', 'band')
- applied: bfloat16 [24576, 32768], P('grid', 'band')
Outputs:
- gram_block: float32 [512, 32768], P('grid', 'band')
- projected: float32 [512, 32768], P('grid', 'band')
All inputs are finite; a program needn't handle non-finite values.
Results may differ from the reference program's by a relative error of at most 0.0003.
Values may be sent and summed in bfloat16 or wider, within the bound.
A program may use at most 64 MiB of HBM per device.

```python
import jax
import jax.numpy as jnp
from jax import lax

BAND_DEV = 2048
GROUP = 256
STEPS = 2
NPTS = 24576
NB = 32768
N_BAND = 16


def make_field(key):
    scale = (NPTS * 1.0) ** (-0.25)
    values = jax.random.normal(key, (NPTS, NB), jnp.float32) * scale
    return values.astype(jnp.bfloat16)


def draw_states(key, part):
    key = jax.random.fold_in(key, 3)
    return make_field(key)


def draw_applied(key, part):
    key = jax.random.fold_in(key, 7)
    return make_field(key)


def setup_inputs(seed: int = 0) -> dict:
    streams_of = jax.random.split(jax.random.key(seed), 3)
    states = draw_states(jax.random.fold_in(streams_of[2], 71), 0)
    applied = draw_applied(jax.random.fold_in(streams_of[2], 71), 0)
    return dict(states=states, applied=applied)


def reference(states, applied):
    xr = states.reshape(NPTS, N_BAND, BAND_DEV)
    hr = applied.reshape(NPTS, N_BAND, BAND_DEV)
    zero = jnp.asarray(0).astype(jnp.int32)

    def block(index):
        own = lax.dynamic_index_in_dim(xr, index, 1, keepdims=False)
        gram_rows = []
        ham_rows = []
        for s in range(STEPS):
            source = ((index - s - 1) % N_BAND).astype(jnp.int32)
            start = (zero + s * GROUP).astype(jnp.int32)
            xs = lax.dynamic_slice(xr, (zero, source, start), (NPTS, 1, GROUP))[:, 0]
            hs = lax.dynamic_slice(hr, (zero, source, start), (NPTS, 1, GROUP))[:, 0]
            gram_rows.append(jnp.dot(xs.T, own, preferred_element_type=jnp.float32))
            ham_rows.append(jnp.dot(hs.T, own, preferred_element_type=jnp.float32))
        return jnp.concatenate(gram_rows, axis=0), jnp.concatenate(ham_rows, axis=0)

    gram_all, ham_all = lax.map(block, jnp.arange(N_BAND, dtype=jnp.int32))
    gram_block = gram_all.transpose(1, 0, 2).reshape(STEPS * GROUP, NB)
    projected = ham_all.transpose(1, 0, 2).reshape(STEPS * GROUP, NB)
    return gram_block, projected
```

```python
import jax
import jax.numpy as jnp
from jax import lax
from jax.experimental import pallas as pl
from jax.experimental.pallas import tpu as pltpu
from jax.sharding import PartitionSpec as P

MESH = pl.DeviceIdType.MESH
GROUP = 256
STEPS = 2
N_BAND = 16
N_Y = 4
ROWS = 32
PIECES = 4
KINDS = 2


def kernel(
    x_ref, h_ref, gram_ref, proj_ref,
    own, group, group_t, part, from_core, from_y, away, from_z,
    own_sem, group_send, group_recv, core_send, core_recv, y_send, y_recv, z_send, z_recv,
):
    width = own.shape[1]
    piece = width // PIECES
    grid_at, band_at = lax.axis_index("grid"), lax.axis_index("band")
    half, y_at, core = grid_at // 8, lax.rem(grid_at // 2, N_Y), lax.rem(grid_at, 2)

    def band(by):
        return {"band": lax.rem(band_at + by + N_BAND, N_BAND)}

    def along_y(by):
        return {"grid": half * 8 + lax.rem(y_at + by, N_Y) * 2 + core}

    sibling = {"grid": grid_at + 1 - 2 * core}
    opposite = {"grid": lax.rem(grid_at + 8, 16)}

    load = pltpu.make_async_copy(x_ref, own, own_sem)
    load.start()

    barrier = pltpu.get_barrier_semaphore()
    partners = [band(1), band(-1), band(2), band(-2), sibling, opposite]
    partners += [along_y(k) for k in range(1, N_Y)]
    for partner in partners:
        pl.semaphore_signal(barrier, inc=1, device_id=partner, device_id_type=MESH)
    pl.semaphore_wait(barrier, len(partners))

    def group_copy(chunk):
        step = (1 - half) if chunk < KINDS else half
        source = x_ref if chunk % KINDS == 0 else h_ref
        low = pl.multiple_of(step * GROUP, GROUP)
        return pltpu.make_async_remote_copy(
            src_ref=source.at[:, pl.ds(low, GROUP)],
            dst_ref=group.at[chunk],
            send_sem=group_send.at[chunk],
            recv_sem=group_recv.at[chunk],
            device_id={"band": lax.rem(band_at + step + 1, N_BAND)},
            device_id_type=MESH,
        )

    def core_copy(chunk, p):
        cols = pl.ds(p * piece, piece)
        return pltpu.make_async_remote_copy(
            src_ref=part.at[chunk, 1 - core, :, :, cols],
            dst_ref=from_core.at[chunk, :, :, cols],
            send_sem=core_send.at[chunk, p],
            recv_sem=core_recv.at[chunk, p],
            device_id=sibling,
            device_id_type=MESH,
        )

    def y_copy(chunk, p, by):
        cols = pl.ds(p * piece, piece)
        return pltpu.make_async_remote_copy(
            src_ref=part.at[chunk, core, lax.rem(y_at + by, N_Y), :, cols],
            dst_ref=from_y.at[chunk, by - 1, :, cols],
            send_sem=y_send.at[chunk, p, by - 1],
            recv_sem=y_recv.at[chunk, p, by - 1],
            device_id=along_y(by),
            device_id_type=MESH,
        )

    def z_copy(kind):
        return pltpu.make_async_remote_copy(
            src_ref=away.at[kind],
            dst_ref=from_z.at[kind],
            send_sem=z_send.at[kind],
            recv_sem=z_recv.at[kind],
            device_id=opposite,
            device_id_type=MESH,
        )

    def multiply(chunk, p):
        cols = pl.ds(p * piece, piece)
        product = jnp.dot(group_t[...], own[:, cols], preferred_element_type=jnp.float32)
        for y in range(N_Y):
            for c in range(2):
                low = (2 * y + c) * ROWS
                part[chunk, c, y, :, cols] = product[low : low + ROWS]
        core_copy(chunk, p).start()

    def pair_sum(chunk, p):
        cols = pl.ds(p * piece, piece)
        core_copy(chunk, p).wait_recv()
        part[chunk, core, :, :, cols] = part[chunk, core, :, :, cols] + from_core[chunk, :, :, cols]
        for by in (2, 1, 3):
            y_copy(chunk, p, by).start()

    def products(chunk):
        group_copy(chunk).wait_recv()
        group_t[...] = group[chunk].T
        for p in range(PIECES):
            multiply(chunk, p)
            if p > 0:
                pair_sum(chunk, p - 1)
        pair_sum(chunk, PIECES - 1)

    def y_sum(chunk, p):
        cols = pl.ds(p * piece, piece)
        for by in range(1, N_Y):
            y_copy(chunk, p, by).wait_recv()
        return (
            part[chunk, core, y_at, :, cols]
            + from_y[chunk, 0, :, cols]
            + from_y[chunk, 1, :, cols]
            + from_y[chunk, 2, :, cols]
        )

    def away_sum(chunk):
        for p in range(PIECES):
            away[chunk, :, pl.ds(p * piece, piece)] = y_sum(chunk, p)

    def home_sum(chunk, out_ref):
        for p in range(PIECES):
            out_ref[:, pl.ds(p * piece, piece)] = y_sum(chunk, p)

    def finish(kind, out_ref):
        z_copy(kind).wait_recv()
        out_ref[...] += from_z[kind]

    group_copy(0).start()
    group_copy(1).start()
    load.wait()
    group_copy(0).wait_send()
    group_copy(2).start()
    products(0)
    group_copy(1).wait_send()
    group_copy(3).start()
    products(1)
    away_sum(0)
    away_sum(1)
    group_copy(2).wait_send()
    z_copy(0).start()
    products(2)
    group_copy(3).wait_send()
    z_copy(1).start()
    products(3)
    home_sum(2, gram_ref)
    home_sum(3, proj_ref)
    finish(0, gram_ref)
    finish(1, proj_ref)

    for chunk in range(KINDS * STEPS):
        for p in range(PIECES):
            core_copy(chunk, p).wait_send()
            for by in range(1, N_Y):
                y_copy(chunk, p, by).wait_send()
    for kind in range(KINDS):
        z_copy(kind).wait_send()


def per_device(states, applied):
    points, width = states.shape
    chunks = KINDS * STEPS
    f32, bf16, dma = jnp.float32, jnp.bfloat16, pltpu.SemaphoreType.DMA
    out = jax.ShapeDtypeStruct((ROWS, width), f32)
    return pl.pallas_call(
        kernel,
        out_shape=(out, out),
        in_specs=[pl.BlockSpec(memory_space=pl.ANY)] * 2,
        out_specs=(pl.BlockSpec(memory_space=pltpu.VMEM),) * 2,
        scratch_shapes=[
            pltpu.VMEM((points, width), bf16),
            pltpu.VMEM((chunks, points, GROUP), bf16),
            pltpu.VMEM((GROUP, points), bf16),
            pltpu.VMEM((chunks, 2, N_Y, ROWS, width), f32),
            pltpu.VMEM((chunks, N_Y, ROWS, width), f32),
            pltpu.VMEM((chunks, N_Y - 1, ROWS, width), f32),
            pltpu.VMEM((KINDS, ROWS, width), f32),
            pltpu.VMEM((KINDS, ROWS, width), f32),
            dma,
            dma((chunks,)),
            dma((chunks,)),
            dma((chunks, PIECES)),
            dma((chunks, PIECES)),
            dma((chunks, PIECES, N_Y - 1)),
            dma((chunks, PIECES, N_Y - 1)),
            dma((KINDS,)),
            dma((KINDS,)),
        ],
        cost_estimate=pl.CostEstimate(
            flops=2 * points * width * GROUP * chunks, bytes_accessed=4 * points * width, transcendentals=0
        ),
        compiler_params=pltpu.CompilerParams(
            collective_id=0, has_side_effects=True, vmem_limit_bytes=48 * 2**20
        ),
        name="ritz_blocks",
    )(states, applied)


def solution(mesh):
    in_specs = (P("grid", "band"), P("grid", "band"))
    out_specs = (P("grid", "band"), P("grid", "band"))
    return jax.shard_map(
        per_device, mesh=mesh, in_specs=in_specs, out_specs=out_specs, check_vma=False
    )
```

```python
import jax
import jax.numpy as jnp
from jax import lax
from jax.experimental import pallas as pl
from jax.experimental.pallas import tpu as pltpu
from jax.sharding import PartitionSpec as P

MESH = pl.DeviceIdType.MESH
GROUP = 256
STEPS = 2
N_BAND = 16
N_Y = 4
N_Z = 4
ROWS = 32
PIECES = 4
SPANS = ((0, 1152), (1152, 384))
KINDS = 2
Z_PARTS = 2
Z_ROWS = ROWS // Z_PARTS


def kernel(
    x_ref, h_ref, gram_ref, proj_ref,
    own, group, group_t, part, from_core, from_y, away, from_z,
    own_sem, group_send, group_recv, core_send, core_recv, y_send, y_recv, z_send, z_recv, go, all_sent,
):
    width = own.shape[1]
    piece = width // PIECES
    grid_at, band_at = lax.axis_index("grid"), lax.axis_index("band")
    half, y_at, core = grid_at // 8, lax.rem(grid_at // 2, N_Y), lax.rem(grid_at, 2)

    def band(by):
        return {"band": lax.rem(band_at + by + N_BAND, N_BAND)}

    def along_y(by):
        return {"grid": half * 8 + lax.rem(y_at + by, N_Y) * 2 + core}

    sibling = {"grid": grid_at + 1 - 2 * core}
    opposite = {"grid": lax.rem(grid_at + 8, 16)}

    pair = {"band": band_at + 1 - 2 * lax.rem(band_at, 2)}
    z_low = lax.rem(band_at, N_Z)
    column = []
    for up in range(2):
        for by in range(N_Z):
            if up or by:
                there = band_at - z_low + lax.rem(z_low + by, N_Z)
                column.append({"grid": lax.rem(grid_at + 8 * up, 16), "band": there})

    load = pltpu.make_async_copy(x_ref, own, own_sem)
    load.start()

    barrier = pltpu.get_barrier_semaphore()
    partners = [band(1), band(-1), band(2), band(-2), sibling] + column
    partners += [along_y(k) for k in range(1, N_Y)]
    for partner in partners:
        pl.semaphore_signal(barrier, inc=1, device_id=partner, device_id_type=MESH)
    pl.semaphore_wait(barrier, len(partners))

    def group_copy(chunk, span):
        step = (1 - half) if chunk < KINDS else half
        source = x_ref if chunk % KINDS == 0 else h_ref
        low = pl.multiple_of(step * GROUP, GROUP)
        points = pl.ds(*SPANS[span])
        return pltpu.make_async_remote_copy(
            src_ref=source.at[points, pl.ds(low, GROUP)],
            dst_ref=group.at[chunk, points],
            send_sem=group_send.at[chunk, span],
            recv_sem=group_recv.at[chunk, span],
            device_id={"band": lax.rem(band_at + step + 1, N_BAND)},
            device_id_type=MESH,
        )

    def core_copy(chunk, p):
        cols = pl.ds(p * piece, piece)
        return pltpu.make_async_remote_copy(
            src_ref=part.at[chunk, 1 - core, :, :, cols],
            dst_ref=from_core.at[chunk, :, :, cols],
            send_sem=core_send.at[chunk, p],
            recv_sem=core_recv.at[chunk, p],
            device_id=sibling,
            device_id_type=MESH,
        )

    def y_copy(chunk, p, by):
        cols = pl.ds(p * piece, piece)
        return pltpu.make_async_remote_copy(
            src_ref=part.at[chunk, core, lax.rem(y_at + by, N_Y), :, cols],
            dst_ref=from_y.at[chunk, by - 1, :, cols],
            send_sem=y_send.at[chunk, p, by - 1],
            recv_sem=y_recv.at[chunk, p, by - 1],
            device_id=along_y(by),
            device_id_type=MESH,
        )

    def z_copy(kind, part_at):
        rows = pl.ds(part_at * Z_ROWS, Z_ROWS)
        return pltpu.make_async_remote_copy(
            src_ref=away.at[kind, rows],
            dst_ref=from_z.at[kind, rows],
            send_sem=z_send.at[kind, part_at],
            recv_sem=z_recv.at[kind, part_at],
            device_id=opposite,
            device_id_type=MESH,
        )

    def transpose(chunk, span):
        points = pl.ds(*SPANS[span])
        group_copy(chunk, span).wait_recv()
        group_t[:, points] = group[chunk, points].T

    def multiply(chunk, p, points, add):
        cols = pl.ds(p * piece, piece)
        product = jnp.dot(
            group_t[:, points], own[points, cols], preferred_element_type=jnp.float32
        )
        for y in range(N_Y):
            for c in range(2):
                low = (2 * y + c) * ROWS
                rows = product[low : low + ROWS]
                part[chunk, c, y, :, cols] = part[chunk, c, y, :, cols] + rows if add else rows

    def pair_sum(chunk, p):
        cols = pl.ds(p * piece, piece)
        core_copy(chunk, p).wait_recv()
        part[chunk, core, :, :, cols] = part[chunk, core, :, :, cols] + from_core[chunk, :, :, cols]
        for by in (2, 1, 3):
            y_copy(chunk, p, by).start()

    def send_pieces(chunk, points, add):
        for p in range(PIECES):
            multiply(chunk, p, points, add)
            core_copy(chunk, p).start()
            if p > 0:
                pair_sum(chunk, p - 1)
        pair_sum(chunk, PIECES - 1)

    def products(chunk):
        for span in range(len(SPANS)):
            transpose(chunk, span)
        send_pieces(chunk, pl.ds(0, own.shape[0]), False)

    def first_products(chunk):
        transpose(chunk, 0)
        for p in range(PIECES):
            multiply(chunk, p, pl.ds(*SPANS[0]), False)

    def last_products(chunk):
        transpose(chunk, 1)
        send_pieces(chunk, pl.ds(*SPANS[1]), True)

    def y_sum(chunk, p):
        cols = pl.ds(p * piece, piece)
        for by in range(1, N_Y):
            y_copy(chunk, p, by).wait_recv()
        return (
            part[chunk, core, y_at, :, cols]
            + from_y[chunk, 0, :, cols]
            + from_y[chunk, 1, :, cols]
            + from_y[chunk, 2, :, cols]
        )

    def away_sum(chunk):
        for p in range(PIECES):
            away[chunk, :, pl.ds(p * piece, piece)] = y_sum(chunk, p)

    def home_sum(chunk, out_ref):
        for p in range(PIECES):
            out_ref[:, pl.ds(p * piece, piece)] = y_sum(chunk, p)

    def finish(kind, out_ref):
        for part_at in range(Z_PARTS):
            rows = pl.ds(part_at * Z_ROWS, Z_ROWS)
            z_copy(kind, part_at).wait_recv()
            out_ref[rows, :] += from_z[kind, rows]

    def start(chunk):
        for span in range(len(SPANS)):
            group_copy(chunk, span).start()

    def sent(chunk):
        for span in range(len(SPANS)):
            group_copy(chunk, span).wait_send()

    start(0)
    start(1)
    load.wait()
    products(0)
    sent(0)
    sent(1)
    pl.semaphore_signal(go, inc=1, device_id=pair, device_id_type=MESH)
    pl.semaphore_wait(go, 1)
    start(2)
    start(3)
    products(1)
    away_sum(0)
    away_sum(1)
    products(2)
    sent(2)
    z_copy(0, 0).start()
    first_products(3)
    sent(3)
    for there in column:
        pl.semaphore_signal(all_sent, inc=1, device_id=there, device_id_type=MESH)
    pl.semaphore_wait(all_sent, len(column))
    z_copy(0, 1).start()
    z_copy(1, 0).start()
    z_copy(1, 1).start()
    last_products(3)
    home_sum(2, gram_ref)
    home_sum(3, proj_ref)
    finish(0, gram_ref)
    finish(1, proj_ref)

    for chunk in range(KINDS * STEPS):
        for p in range(PIECES):
            core_copy(chunk, p).wait_send()
            for by in range(1, N_Y):
                y_copy(chunk, p, by).wait_send()
    for kind in range(KINDS):
        for part_at in range(Z_PARTS):
            z_copy(kind, part_at).wait_send()


def per_device(states, applied):
    points, width = states.shape
    chunks = KINDS * STEPS
    f32, bf16, dma = jnp.float32, jnp.bfloat16, pltpu.SemaphoreType.DMA
    out = jax.ShapeDtypeStruct((ROWS, width), f32)
    return pl.pallas_call(
        kernel,
        out_shape=(out, out),
        in_specs=[pl.BlockSpec(memory_space=pl.ANY)] * 2,
        out_specs=(pl.BlockSpec(memory_space=pltpu.VMEM),) * 2,
        scratch_shapes=[
            pltpu.VMEM((points, width), bf16),
            pltpu.VMEM((chunks, points, GROUP), bf16),
            pltpu.VMEM((GROUP, points), bf16),
            pltpu.VMEM((chunks, 2, N_Y, ROWS, width), f32),
            pltpu.VMEM((chunks, N_Y, ROWS, width), f32),
            pltpu.VMEM((chunks, N_Y - 1, ROWS, width), f32),
            pltpu.VMEM((KINDS, ROWS, width), f32),
            pltpu.VMEM((KINDS, ROWS, width), f32),
            dma,
            dma((chunks, len(SPANS))),
            dma((chunks, len(SPANS))),
            dma((chunks, PIECES)),
            dma((chunks, PIECES)),
            dma((chunks, PIECES, N_Y - 1)),
            dma((chunks, PIECES, N_Y - 1)),
            dma((KINDS, Z_PARTS)),
            dma((KINDS, Z_PARTS)),
            pltpu.SemaphoreType.REGULAR,
            pltpu.SemaphoreType.REGULAR,
        ],
        cost_estimate=pl.CostEstimate(
            flops=2 * points * width * GROUP * chunks, bytes_accessed=4 * points * width, transcendentals=0
        ),
        compiler_params=pltpu.CompilerParams(
            collective_id=0, has_side_effects=True, vmem_limit_bytes=48 * 2**20
        ),
        name="ritz_blocks",
    )(states, applied)


def solution(mesh):
    in_specs = (P("grid", "band"), P("grid", "band"))
    out_specs = (P("grid", "band"), P("grid", "band"))
    return jax.shard_map(
        per_device, mesh=mesh, in_specs=in_specs, out_specs=out_specs, check_vma=False
    )
```

```python
import jax
import jax.numpy as jnp
from jax import lax
from jax.experimental import pallas as pl
from jax.experimental.pallas import tpu as pltpu
from jax.sharding import PartitionSpec as P

MESH = pl.DeviceIdType.MESH
GROUP = 256
STEPS = 2
N_BAND = 16
N_Y = 4
N_Z = 4
ROWS = 32
PIECES = 4
SPANS = ((0, 1024), (1024, 256), (1280, 256))
KINDS = 2
Z_PARTS = 2
LEVELS = 255.0
POWER = 31.25
LOG_LOW = -125.0 * 0.6931471805599453
TINY = 1e-37
Z_ROWS = ROWS // Z_PARTS


def kernel(
    x_ref, h_ref, gram_ref, proj_ref,
    own, group, group_t, part, from_core, from_y, away, code, from_z, unit, from_unit,
    own_sem, group_send, group_recv, core_send, core_recv, y_send, y_recv, z_send, z_recv, unit_send, unit_recv, go, all_sent,
):
    width = own.shape[1]
    piece = width // PIECES
    grid_at, band_at = lax.axis_index("grid"), lax.axis_index("band")
    half, y_at, core = grid_at // 8, lax.rem(grid_at // 2, N_Y), lax.rem(grid_at, 2)

    def band(by):
        return {"band": lax.rem(band_at + by + N_BAND, N_BAND)}

    def along_y(by):
        return {"grid": half * 8 + lax.rem(y_at + by, N_Y) * 2 + core}

    sibling = {"grid": grid_at + 1 - 2 * core}
    opposite = {"grid": lax.rem(grid_at + 8, 16)}

    pair = {"band": band_at + 1 - 2 * lax.rem(band_at, 2)}
    z_low = lax.rem(band_at, N_Z)
    column = []
    for up in range(2):
        for by in range(N_Z):
            if up or by:
                there = band_at - z_low + lax.rem(z_low + by, N_Z)
                column.append({"grid": lax.rem(grid_at + 8 * up, 16), "band": there})

    load = pltpu.make_async_copy(x_ref, own, own_sem)
    load.start()

    barrier = pltpu.get_barrier_semaphore()
    partners = [band(1), band(-1), band(2), band(-2), sibling] + column
    partners += [along_y(k) for k in range(1, N_Y)]
    for partner in partners:
        pl.semaphore_signal(barrier, inc=1, device_id=partner, device_id_type=MESH)
    pl.semaphore_wait(barrier, len(partners))

    def group_copy(chunk, span):
        step = (1 - half) if chunk < KINDS else half
        source = x_ref if chunk % KINDS == 0 else h_ref
        low = pl.multiple_of(step * GROUP, GROUP)
        points = pl.ds(*SPANS[span])
        return pltpu.make_async_remote_copy(
            src_ref=source.at[points, pl.ds(low, GROUP)],
            dst_ref=group.at[chunk, points],
            send_sem=group_send.at[chunk, span],
            recv_sem=group_recv.at[chunk, span],
            device_id={"band": lax.rem(band_at + step + 1, N_BAND)},
            device_id_type=MESH,
        )

    def core_copy(chunk, p):
        cols = pl.ds(p * piece, piece)
        return pltpu.make_async_remote_copy(
            src_ref=part.at[chunk, 1 - core, :, :, cols],
            dst_ref=from_core.at[chunk, :, :, cols],
            send_sem=core_send.at[chunk, p],
            recv_sem=core_recv.at[chunk, p],
            device_id=sibling,
            device_id_type=MESH,
        )

    def y_copy(chunk, p, by):
        cols = pl.ds(p * piece, piece)
        return pltpu.make_async_remote_copy(
            src_ref=part.at[chunk, core, lax.rem(y_at + by, N_Y), :, cols],
            dst_ref=from_y.at[chunk, by - 1, :, cols],
            send_sem=y_send.at[chunk, p, by - 1],
            recv_sem=y_recv.at[chunk, p, by - 1],
            device_id=along_y(by),
            device_id_type=MESH,
        )

    def z_copy(kind, part_at):
        rows = pl.ds(part_at * Z_ROWS, Z_ROWS)
        return pltpu.make_async_remote_copy(
            src_ref=code.at[kind, rows],
            dst_ref=from_z.at[kind, rows],
            send_sem=z_send.at[kind, part_at],
            recv_sem=z_recv.at[kind, part_at],
            device_id=opposite,
            device_id_type=MESH,
        )

    def unit_copy():
        return pltpu.make_async_remote_copy(
            src_ref=unit,
            dst_ref=from_unit,
            send_sem=unit_send,
            recv_sem=unit_recv,
            device_id=opposite,
            device_id_type=MESH,
        )

    def encode(kind):
        largest = jnp.max(jnp.abs(away[kind]), axis=(0, 1), keepdims=True)
        sixteenth = jnp.maximum(largest * 0.0625, TINY)
        unit[kind] = jnp.broadcast_to(sixteenth, unit.shape[1:])
        inverse = 1.0 / sixteenth
        for p in range(PIECES):
            cols = pl.ds(p * piece, piece)
            value = away[kind, :, cols]
            level = jnp.abs(value) * 0.0625 * inverse
            size = jnp.exp(POWER * jnp.log(1.0 + LEVELS * level) + LOG_LOW)
            code[kind, :, cols] = jnp.where(value < 0, -size, size).astype(jnp.bfloat16)

    def decode(kind, rows, cols):
        got = from_z[kind, rows, cols].astype(jnp.float32)
        level = (jnp.exp((jnp.log(jnp.abs(got)) - LOG_LOW) * (1.0 / POWER)) - 1.0) * (1.0 / LEVELS)
        size = level * (from_unit[kind, 0:1, 0:1] * 16.0)
        return jnp.where(got < 0, -size, size)

    def transpose(chunk, span):
        points = pl.ds(*SPANS[span])
        group_copy(chunk, span).wait_recv()
        group_t[:, points] = group[chunk, points].T

    def multiply(chunk, p, points, add):
        cols = pl.ds(p * piece, piece)
        product = jnp.dot(
            group_t[:, points], own[points, cols], preferred_element_type=jnp.float32
        )
        for y in range(N_Y):
            for c in range(2):
                low = (2 * y + c) * ROWS
                rows = product[low : low + ROWS]
                part[chunk, c, y, :, cols] = part[chunk, c, y, :, cols] + rows if add else rows

    def pair_sum(chunk, p):
        cols = pl.ds(p * piece, piece)
        core_copy(chunk, p).wait_recv()
        part[chunk, core, :, :, cols] = part[chunk, core, :, :, cols] + from_core[chunk, :, :, cols]
        for by in (2, 1, 3):
            y_copy(chunk, p, by).start()

    def send_pieces(chunk, points, add):
        for p in range(PIECES):
            multiply(chunk, p, points, add)
            core_copy(chunk, p).start()
            if p > 0:
                pair_sum(chunk, p - 1)
        pair_sum(chunk, PIECES - 1)

    def products(chunk):
        for span in range(len(SPANS)):
            transpose(chunk, span)
        send_pieces(chunk, pl.ds(0, own.shape[0]), False)

    def first_products(chunk):
        transpose(chunk, 0)
        transpose(chunk, 1)
        for p in range(PIECES):
            multiply(chunk, p, pl.ds(0, SPANS[2][0]), False)

    def last_products(chunk):
        transpose(chunk, 2)
        send_pieces(chunk, pl.ds(*SPANS[2]), True)

    def y_sum(chunk, p):
        cols = pl.ds(p * piece, piece)
        for by in range(1, N_Y):
            y_copy(chunk, p, by).wait_recv()
        return (
            part[chunk, core, y_at, :, cols]
            + from_y[chunk, 0, :, cols]
            + from_y[chunk, 1, :, cols]
            + from_y[chunk, 2, :, cols]
        )

    def away_sum(chunk):
        for p in range(PIECES):
            away[chunk, :, pl.ds(p * piece, piece)] = y_sum(chunk, p)
        encode(chunk)

    def home_sum(chunk, out_ref):
        for p in range(PIECES):
            out_ref[:, pl.ds(p * piece, piece)] = y_sum(chunk, p)

    def finish(kind, out_ref):
        if kind == 0:
            unit_copy().wait_recv()
        for part_at in range(Z_PARTS):
            rows = pl.ds(part_at * Z_ROWS, Z_ROWS)
            z_copy(kind, part_at).wait_recv()
            for p in range(PIECES):
                cols = pl.ds(p * piece, piece)
                out_ref[rows, cols] += decode(kind, rows, cols)

    def start(chunk):
        for span in range(len(SPANS)):
            group_copy(chunk, span).start()

    def sent(chunk):
        for span in range(len(SPANS)):
            group_copy(chunk, span).wait_send()

    start(0)
    start(1)
    load.wait()
    products(0)
    sent(0)
    sent(1)
    pl.semaphore_signal(go, inc=1, device_id=pair, device_id_type=MESH)
    late = jnp.logical_or(
        jnp.logical_and(half == 0, z_low == N_Z - 1), jnp.logical_and(half == 1, z_low == 0)
    )
    @pl.when(late)
    def _():
        pl.semaphore_wait(go, 1)
    start(2)
    start(3)
    products(1)
    away_sum(0)
    away_sum(1)
    @pl.when(jnp.logical_not(late))
    def _():
        pl.semaphore_wait(go, 1)
    products(2)
    first_products(3)
    sent(2)
    sent(3)
    for there in column:
        pl.semaphore_signal(all_sent, inc=1, device_id=there, device_id_type=MESH)
    last_products(3)
    pl.semaphore_wait(all_sent, len(column))
    unit_copy().start()
    z_copy(0, 0).start()
    z_copy(0, 1).start()
    z_copy(1, 0).start()
    z_copy(1, 1).start()
    home_sum(2, gram_ref)
    home_sum(3, proj_ref)
    finish(0, gram_ref)
    finish(1, proj_ref)

    for chunk in range(KINDS * STEPS):
        for p in range(PIECES):
            core_copy(chunk, p).wait_send()
            for by in range(1, N_Y):
                y_copy(chunk, p, by).wait_send()
    unit_copy().wait_send()
    for kind in range(KINDS):
        for part_at in range(Z_PARTS):
            z_copy(kind, part_at).wait_send()


def per_device(states, applied):
    points, width = states.shape
    chunks = KINDS * STEPS
    f32, bf16, dma = jnp.float32, jnp.bfloat16, pltpu.SemaphoreType.DMA
    out = jax.ShapeDtypeStruct((ROWS, width), f32)
    return pl.pallas_call(
        kernel,
        out_shape=(out, out),
        in_specs=[pl.BlockSpec(memory_space=pl.ANY)] * 2,
        out_specs=(pl.BlockSpec(memory_space=pltpu.VMEM),) * 2,
        scratch_shapes=[
            pltpu.VMEM((points, width), bf16),
            pltpu.VMEM((chunks, points, GROUP), bf16),
            pltpu.VMEM((GROUP, points), bf16),
            pltpu.VMEM((chunks, 2, N_Y, ROWS, width), f32),
            pltpu.VMEM((chunks, N_Y, ROWS, width), f32),
            pltpu.VMEM((chunks, N_Y - 1, ROWS, width), f32),
            pltpu.VMEM((KINDS, ROWS, width), f32),
            pltpu.VMEM((KINDS, ROWS, width), bf16),
            pltpu.VMEM((KINDS, ROWS, width), bf16),
            pltpu.VMEM((KINDS, 8, 128), f32),
            pltpu.VMEM((KINDS, 8, 128), f32),
            dma,
            dma((chunks, len(SPANS))),
            dma((chunks, len(SPANS))),
            dma((chunks, PIECES)),
            dma((chunks, PIECES)),
            dma((chunks, PIECES, N_Y - 1)),
            dma((chunks, PIECES, N_Y - 1)),
            dma((KINDS, Z_PARTS)),
            dma((KINDS, Z_PARTS)),
            dma,
            dma,
            pltpu.SemaphoreType.REGULAR,
            pltpu.SemaphoreType.REGULAR,
        ],
        cost_estimate=pl.CostEstimate(
            flops=2 * points * width * GROUP * chunks, bytes_accessed=4 * points * width, transcendentals=0
        ),
        compiler_params=pltpu.CompilerParams(
            collective_id=0, has_side_effects=True, vmem_limit_bytes=48 * 2**20
        ),
        name="ritz_blocks",
    )(states, applied)


def solution(mesh):
    in_specs = (P("grid", "band"), P("grid", "band"))
    out_specs = (P("grid", "band"), P("grid", "band"))
    return jax.shard_map(
        per_device, mesh=mesh, in_specs=in_specs, out_specs=out_specs, check_vma=False
    )
```

```python
import jax
import jax.numpy as jnp
from jax import lax
from jax.experimental import pallas as pl
from jax.experimental.pallas import tpu as pltpu
from jax.sharding import PartitionSpec as P

MESH = pl.DeviceIdType.MESH
GROUP = 256
STEPS = 2
N_BAND = 16
N_Y = 4
N_Z = 4
ROWS = 32
PIECES = 2
SPANS = ((0, 1024), (1024, 256), (1280, 256))
KINDS = 2
Z_PARTS = 2
LEVELS = 255.0
POWER = 31.25
LOG_LOW = -125.0 * 0.6931471805599453
TINY = 1e-37
Z_ROWS = ROWS // Z_PARTS


def kernel(
    x_ref, h_ref, gram_ref, proj_ref,
    own, group, group_t, part, from_core, from_y, away, code, from_z, unit, from_unit,
    own_sem, group_send, group_recv, core_send, core_recv, y_send, y_recv, z_send, z_recv, unit_send, unit_recv, go, go_on, all_sent,
):
    width = own.shape[1]
    piece = width // PIECES
    grid_at, band_at = lax.axis_index("grid"), lax.axis_index("band")
    half, y_at, core = grid_at // 8, lax.rem(grid_at // 2, N_Y), lax.rem(grid_at, 2)

    def band(by):
        return {"band": lax.rem(band_at + by + N_BAND, N_BAND)}

    def along_y(by):
        return {"grid": half * 8 + lax.rem(y_at + by, N_Y) * 2 + core}

    sibling = {"grid": grid_at + 1 - 2 * core}
    opposite = {"grid": lax.rem(grid_at + 8, 16)}

    beside = band_at + 1 - 2 * lax.rem(band_at, 2)
    pair = [{"grid": grid_at, "band": beside}, {"grid": sibling["grid"], "band": beside}]
    z_low = lax.rem(band_at, N_Z)
    column = []
    for up in range(2):
        for by in range(N_Z):
            if up or by:
                there = band_at - z_low + lax.rem(z_low + by, N_Z)
                column.append({"grid": lax.rem(grid_at + 8 * up, 16), "band": there})

    load = pltpu.make_async_copy(x_ref, own, own_sem)
    load.start()

    barrier = pltpu.get_barrier_semaphore()
    partners = [band(1), band(-1), band(2), band(-2), sibling] + pair + column
    partners += [along_y(k) for k in range(1, N_Y)]
    for partner in partners:
        pl.semaphore_signal(barrier, inc=1, device_id=partner, device_id_type=MESH)
    pl.semaphore_wait(barrier, len(partners))

    def group_copy(chunk, span):
        step = (1 - half) if chunk < KINDS else half
        source = x_ref if chunk % KINDS == 0 else h_ref
        low = pl.multiple_of(step * GROUP, GROUP)
        points = pl.ds(*SPANS[span])
        return pltpu.make_async_remote_copy(
            src_ref=source.at[points, pl.ds(low, GROUP)],
            dst_ref=group.at[chunk, points],
            send_sem=group_send.at[chunk, span],
            recv_sem=group_recv.at[chunk, span],
            device_id={"band": lax.rem(band_at + step + 1, N_BAND)},
            device_id_type=MESH,
        )

    def core_copy(chunk, p):
        cols = pl.ds(p * piece, piece)
        return pltpu.make_async_remote_copy(
            src_ref=part.at[chunk, 1 - core, :, :, cols],
            dst_ref=from_core.at[chunk, :, :, cols],
            send_sem=core_send.at[chunk, p],
            recv_sem=core_recv.at[chunk, p],
            device_id=sibling,
            device_id_type=MESH,
        )

    def y_copy(chunk, p, by):
        cols = pl.ds(p * piece, piece)
        return pltpu.make_async_remote_copy(
            src_ref=part.at[chunk, core, lax.rem(y_at + by, N_Y), :, cols],
            dst_ref=from_y.at[chunk, by - 1, :, cols],
            send_sem=y_send.at[chunk, p, by - 1],
            recv_sem=y_recv.at[chunk, p, by - 1],
            device_id=along_y(by),
            device_id_type=MESH,
        )

    def z_copy(kind, part_at):
        rows = pl.ds(part_at * Z_ROWS, Z_ROWS)
        return pltpu.make_async_remote_copy(
            src_ref=code.at[kind, rows],
            dst_ref=from_z.at[kind, rows],
            send_sem=z_send.at[kind, part_at],
            recv_sem=z_recv.at[kind, part_at],
            device_id=opposite,
            device_id_type=MESH,
        )

    def unit_copy():
        return pltpu.make_async_remote_copy(
            src_ref=unit,
            dst_ref=from_unit,
            send_sem=unit_send,
            recv_sem=unit_recv,
            device_id=opposite,
            device_id_type=MESH,
        )

    def encode(kind):
        largest = jnp.max(jnp.abs(away[kind]), axis=(0, 1), keepdims=True)
        sixteenth = jnp.maximum(largest * 0.0625, TINY)
        unit[kind] = jnp.broadcast_to(sixteenth, unit.shape[1:])
        inverse = 1.0 / sixteenth
        for p in range(PIECES):
            cols = pl.ds(p * piece, piece)
            value = away[kind, :, cols]
            level = jnp.abs(value) * 0.0625 * inverse
            size = jnp.exp(POWER * jnp.log(1.0 + LEVELS * level) + LOG_LOW)
            code[kind, :, cols] = jnp.where(value < 0, -size, size).astype(jnp.bfloat16)

    def decode(kind, rows, cols):
        got = from_z[kind, rows, cols].astype(jnp.float32)
        level = (jnp.exp((jnp.log(jnp.abs(got)) - LOG_LOW) * (1.0 / POWER)) - 1.0) * (1.0 / LEVELS)
        size = level * (from_unit[kind, 0:1, 0:1] * 16.0)
        return jnp.where(got < 0, -size, size)

    def transpose(chunk, span):
        points = pl.ds(*SPANS[span])
        group_copy(chunk, span).wait_recv()
        group_t[:, points] = group[chunk, points].T

    def multiply(chunk, p, points, add):
        cols = pl.ds(p * piece, piece)
        product = jnp.dot(
            group_t[:, points], own[points, cols], preferred_element_type=jnp.float32
        )
        for y in range(N_Y):
            for c in range(2):
                low = (2 * y + c) * ROWS
                rows = product[low : low + ROWS]
                part[chunk, c, y, :, cols] = part[chunk, c, y, :, cols] + rows if add else rows

    def pair_sum(chunk, p):
        cols = pl.ds(p * piece, piece)
        core_copy(chunk, p).wait_recv()
        part[chunk, core, :, :, cols] = part[chunk, core, :, :, cols] + from_core[chunk, :, :, cols]
        for by in (2, 1, 3):
            y_copy(chunk, p, by).start()

    def send_pieces(chunk, points, add):
        for p in range(PIECES):
            multiply(chunk, p, points, add)
            core_copy(chunk, p).start()
            if p > 0:
                pair_sum(chunk, p - 1)
        pair_sum(chunk, PIECES - 1)

    def products(chunk):
        for span in range(len(SPANS)):
            transpose(chunk, span)
        send_pieces(chunk, pl.ds(0, own.shape[0]), False)

    def first_products(chunk):
        transpose(chunk, 0)
        transpose(chunk, 1)
        for p in range(PIECES):
            multiply(chunk, p, pl.ds(0, SPANS[2][0]), False)

    def last_products(chunk):
        transpose(chunk, 2)
        send_pieces(chunk, pl.ds(*SPANS[2]), True)

    def y_sum(chunk, p):
        cols = pl.ds(p * piece, piece)
        for by in range(1, N_Y):
            y_copy(chunk, p, by).wait_recv()
        return (
            part[chunk, core, y_at, :, cols]
            + from_y[chunk, 0, :, cols]
            + from_y[chunk, 1, :, cols]
            + from_y[chunk, 2, :, cols]
        )

    def away_sum(chunk):
        for p in range(PIECES):
            away[chunk, :, pl.ds(p * piece, piece)] = y_sum(chunk, p)
        encode(chunk)

    def home_sum(chunk, out_ref):
        for p in range(PIECES):
            out_ref[:, pl.ds(p * piece, piece)] = y_sum(chunk, p)

    def finish(kind, out_ref):
        if kind == 0:
            unit_copy().wait_recv()
        for part_at in range(Z_PARTS):
            rows = pl.ds(part_at * Z_ROWS, Z_ROWS)
            z_copy(kind, part_at).wait_recv()
            for p in range(PIECES):
                cols = pl.ds(p * piece, piece)
                out_ref[rows, cols] += decode(kind, rows, cols)

    def start(chunk):
        for span in range(len(SPANS)):
            group_copy(chunk, span).start()

    def sent(chunk):
        for span in range(len(SPANS)):
            group_copy(chunk, span).wait_send()

    start(0)
    start(1)
    load.wait()
    products(0)
    sent(0)
    group_copy(1, 0).wait_send()
    group_copy(1, 1).wait_send()
    for there in pair:
        pl.semaphore_signal(go, inc=1, device_id=there, device_id_type=MESH)
    group_copy(1, 2).wait_send()
    for there in pair:
        pl.semaphore_signal(go_on, inc=1, device_id=there, device_id_type=MESH)
    late = jnp.logical_or(
        jnp.logical_and(half == 0, z_low == N_Z - 1), jnp.logical_and(half == 1, z_low == 0)
    )
    @pl.when(late)
    def _():
        pl.semaphore_wait(go, 2)
    group_copy(2, 2).start()
    @pl.when(late)
    def _():
        pl.semaphore_wait(go_on, 2)
    group_copy(2, 0).start()
    group_copy(2, 1).start()
    start(3)
    products(1)
    away_sum(0)
    away_sum(1)
    @pl.when(jnp.logical_not(late))
    def _():
        pl.semaphore_wait(go, 2)
        pl.semaphore_wait(go_on, 2)
    products(2)
    first_products(3)
    sent(2)
    sent(3)
    for there in column:
        pl.semaphore_signal(all_sent, inc=1, device_id=there, device_id_type=MESH)
    last_products(3)
    home_sum(2, gram_ref)
    pl.semaphore_wait(all_sent, len(column))
    unit_copy().start()
    z_copy(0, 0).start()
    z_copy(0, 1).start()
    z_copy(1, 0).start()
    z_copy(1, 1).start()
    home_sum(3, proj_ref)
    finish(0, gram_ref)
    finish(1, proj_ref)

    for chunk in range(KINDS * STEPS):
        for p in range(PIECES):
            core_copy(chunk, p).wait_send()
            for by in range(1, N_Y):
                y_copy(chunk, p, by).wait_send()
    unit_copy().wait_send()
    for kind in range(KINDS):
        for part_at in range(Z_PARTS):
            z_copy(kind, part_at).wait_send()


def per_device(states, applied):
    points, width = states.shape
    chunks = KINDS * STEPS
    f32, bf16, dma = jnp.float32, jnp.bfloat16, pltpu.SemaphoreType.DMA
    out = jax.ShapeDtypeStruct((ROWS, width), f32)
    return pl.pallas_call(
        kernel,
        out_shape=(out, out),
        in_specs=[pl.BlockSpec(memory_space=pl.ANY)] * 2,
        out_specs=(pl.BlockSpec(memory_space=pltpu.VMEM),) * 2,
        scratch_shapes=[
            pltpu.VMEM((points, width), bf16),
            pltpu.VMEM((chunks, points, GROUP), bf16),
            pltpu.VMEM((GROUP, points), bf16),
            pltpu.VMEM((chunks, 2, N_Y, ROWS, width), f32),
            pltpu.VMEM((chunks, N_Y, ROWS, width), f32),
            pltpu.VMEM((chunks, N_Y - 1, ROWS, width), f32),
            pltpu.VMEM((KINDS, ROWS, width), f32),
            pltpu.VMEM((KINDS, ROWS, width), bf16),
            pltpu.VMEM((KINDS, ROWS, width), bf16),
            pltpu.VMEM((KINDS, 8, 128), f32),
            pltpu.VMEM((KINDS, 8, 128), f32),
            dma,
            dma((chunks, len(SPANS))),
            dma((chunks, len(SPANS))),
            dma((chunks, PIECES)),
            dma((chunks, PIECES)),
            dma((chunks, PIECES, N_Y - 1)),
            dma((chunks, PIECES, N_Y - 1)),
            dma((KINDS, Z_PARTS)),
            dma((KINDS, Z_PARTS)),
            dma,
            dma,
            pltpu.SemaphoreType.REGULAR,
            pltpu.SemaphoreType.REGULAR,
            pltpu.SemaphoreType.REGULAR,
        ],
        cost_estimate=pl.CostEstimate(
            flops=2 * points * width * GROUP * chunks, bytes_accessed=4 * points * width, transcendentals=0
        ),
        compiler_params=pltpu.CompilerParams(
            collective_id=0, has_side_effects=True, vmem_limit_bytes=48 * 2**20
        ),
        name="ritz_blocks",
    )(states, applied)


def solution(mesh):
    in_specs = (P("grid", "band"), P("grid", "band"))
    out_specs = (P("grid", "band"), P("grid", "band"))
    return jax.shard_map(
        per_device, mesh=mesh, in_specs=in_specs, out_specs=out_specs, check_vma=False
    )
```
